256 devices in a mesh: lat: 8 (over x_hi, y), lon: 32 (over x_lo, z, core).
Axes of the slice: x: 4 (x_hi: 2, x_lo: 2; x = x_hi * 2 + x_lo), y: 4, z: 8, core: 2. Of those that a mesh axis runs over, the one named last changes fastest.
Arguments:
- inputs: bfloat16 [720, 1440, 256], P('lat', 'lon'), may hold values from -6 to 6
- kernel: bfloat16 [3, 3, 256, 256], replicated, may hold values from -0.125 to 0.125
- cotangent: bfloat16 [720, 1440, 256], P('lat', 'lon'), may hold values from -6 to 6
Outputs:
- outputs: bfloat16 [720, 1440, 256], P('lat', 'lon')
- input_grad: bfloat16 [720, 1440, 256], P('lat', 'lon')
- kernel_grad: float32 [3, 3, 256, 256], replicated
The draws below stay inside these ranges and needn't reach their ends.
All inputs are finite; a program needn't handle non-finite values.
Results may differ from the reference program's by a relative error of at most 0.001.
Values may be sent and summed in bfloat16 or wider, within the bound.
A program may use at most 192 MiB of HBM per device.

```python
import math
import jax
import jax.numpy as jnp

CH = 256
NLAT = 720
NLON = 1440


def steps_of(stream_key, shape, shards, least, top_value):
    factor_of = 1.0
    for position, parts in shards:
        heights = jax.random.uniform(jax.random.fold_in(jax.random.fold_in(stream_key, 6), position), (parts,), jnp.float32, least / len(shards), top_value / len(shards))
        factor_of = factor_of * jnp.repeat(jnp.exp(heights), shape[position] // parts).reshape((-1,) + (1,) * (len(shape) - 1 - position))
    return factor_of


def centred(key, shape, scale, limit, pieces=(), dtype=jnp.bfloat16):
    loudness = steps_of(key, shape, pieces, -0.22, 0.18) if pieces else 1.0
    values = jax.random.normal(key, shape, jnp.float32) * scale * loudness
    return jnp.minimum(jnp.maximum(values, -limit), limit).astype(dtype)


def setup_inputs(seed: int = 0) -> dict:
    splits = jax.random.split(jax.random.key(seed), 4)
    inputs = centred(splits[0], (NLAT, NLON, CH), 1.0, 6.0, ((0, 8), (1, 32)))
    kernel = centred(splits[1], (3, 3, CH, CH), (9 * CH) ** -0.5, 0.125)
    cotangent = centred(splits[2], (NLAT, NLON, CH), 1.0, 6.0, ((0, 8), (1, 32)))
    return dict(inputs=inputs, kernel=kernel, cotangent=cotangent)


def pole_pad(field):
    half = NLON // 2
    top = jnp.roll(field[0], -half, axis=0)[None]
    bottom = jnp.roll(field[-1], -half, axis=0)[None]
    rows = jnp.concatenate([top, field, bottom], 0)
    return jnp.concatenate([rows[:, -1:], rows, rows[:, :1]], 1)

def reference(inputs, kernel, cotangent):
    padded = pole_pad(inputs)
    flat_grad = cotangent.reshape(-1, CH)
    result = jnp.zeros((NLAT * NLON, CH), jnp.float32)
    pad_grad = jnp.zeros((NLAT + 2, NLON + 2, CH), jnp.float32)
    taps = []
    for row_tap in range(3):
        for col_tap in range(3):
            window = padded[row_tap:row_tap + NLAT, col_tap:col_tap + NLON].reshape(-1, CH)
            result = result + jnp.dot(window, kernel[row_tap, col_tap], preferred_element_type=jnp.float32)
            taps.append(jnp.dot(window.T, flat_grad, preferred_element_type=jnp.float32))
            spread = jnp.dot(flat_grad, kernel[row_tap, col_tap].T, preferred_element_type=jnp.float32)
            pad_grad = pad_grad.at[row_tap:row_tap + NLAT, col_tap:col_tap + NLON].add(spread.reshape(NLAT, NLON, CH))
    outputs = result.reshape(NLAT, NLON, CH).astype(jnp.bfloat16)
    kernel_grad = jnp.stack(taps).reshape(3, 3, CH, CH) * (1.0 / math.sqrt(NLAT * NLON))
    inner = pad_grad[:, 1:-1]
    inner = inner.at[:, -1].add(pad_grad[:, 0])
    inner = inner.at[:, 0].add(pad_grad[:, -1])
    half = NLON // 2
    grad = inner[1:-1]
    grad = grad.at[0].add(jnp.roll(inner[0], half, axis=0))
    grad = grad.at[-1].add(jnp.roll(inner[-1], half, axis=0))
    return (outputs, grad.astype(jnp.bfloat16), kernel_grad)
```

```python
import functools
import math

import jax
import jax.numpy as jnp
from jax import lax
from jax.experimental import pallas as pl
from jax.experimental.pallas import tpu as pltpu
from jax.sharding import PartitionSpec as P

MESH = pl.DeviceIdType.MESH
F32 = jnp.float32
BF16 = jnp.bfloat16

ROWS, COLS, CH = 90, 45, 256
PITCH = 48
FLAT = (ROWS + 2) * PITCH + 32
DEPTH = 4352
NX, NY, NZ = 4, 4, 8
TILE = 15
TILES = ROWS // TILE
TAPS = 9
GAP = 2
STEPS = TAPS + 2 * TILES


def rows_at(row, count):
    return pl.ds(pl.multiple_of(row * PITCH, 16), count)


def kernel(
    scale,
    x_hbm, w_hbm, c_hbm,
    out_hbm, grad_hbm, kg_hbm,
    x_in, c_in, w,
    xs, cs, xt, x_rows, c_rows, c_halo,
    col_send, col_recv,
    out_v, grad_v,
    term, pair_recv, half, recv1, sum1, recv2, recv3, final,
    load_sem, store_sem, kg_sem,
    row_send_sem, row_recv_sem, col_send_sem, col_recv_sem,
    ar_send_sem, ar_recv_sem,
):
    lat, lon = lax.axis_index("lat"), lax.axis_index("lon")
    x_hi, y = lat // 4, lat % 4
    x_lo, z, core = lon // 16, (lon // 2) % 8, lon % 2
    xc = x_hi * 2 + x_lo

    def device(xx, yy, zz, cc):
        return ((xx // 2) * 4 + yy, ((xx % 2) * 8 + zz) * 2 + cc)

    north, south = lat == 0, lat == 7
    across = (lon + 16) % 32
    up = (jnp.where(north, 0, lat - 1), jnp.where(north, across, lon))
    down = (jnp.where(south, 7, lat + 1), jnp.where(south, across, lon))
    left, right = (lat, (lon + 31) % 32), (lat, (lon + 1) % 32)
    other = device(xc, y, z, 1 - core)

    loads = [
        pltpu.make_async_copy(c_hbm, c_in, load_sem.at[0]),
        pltpu.make_async_copy(x_hbm, x_in, load_sem.at[1]),
        pltpu.make_async_copy(w_hbm, w, load_sem.at[2]),
    ]
    for load in loads:
        load.start()

    barrier = pltpu.get_barrier_semaphore()
    friends = [up, down, left, right, other]
    friends += [device((xc + d) % NX, y, z, core) for d in range(1, NX)]
    friends += [device(xc, (y + d) % NY, z, core) for d in range(1, NY)]
    friends += [device(xc, y, (z + d) % NZ, core) for d in range(1, NZ)]
    for friend in friends:
        pl.semaphore_signal(barrier, inc=1, device_id=friend, device_id_type=MESH)
    pl.semaphore_wait(barrier, len(friends))

    def row_copies(which, source, target):
        to_up, to_down = jnp.where(north, 0, 1), jnp.where(south, 1, 0)
        return [
            pltpu.make_async_remote_copy(
                src_ref=source.at[0], dst_ref=target.at[to_up],
                send_sem=row_send_sem.at[which, 0], recv_sem=row_recv_sem.at[which, to_up],
                device_id=up, device_id_type=MESH,
            ),
            pltpu.make_async_remote_copy(
                src_ref=source.at[ROWS - 1], dst_ref=target.at[to_down],
                send_sem=row_send_sem.at[which, 1], recv_sem=row_recv_sem.at[which, to_down],
                device_id=down, device_id_type=MESH,
            ),
        ]

    def row_wait(which, target):
        for side in range(2):
            pltpu.make_async_copy(target.at[side], target.at[side], row_recv_sem.at[which, side]).wait()

    def col_copies(which):
        return [
            pltpu.make_async_remote_copy(
                src_ref=col_send.at[which, side], dst_ref=col_recv.at[which, side],
                send_sem=col_send_sem.at[which, side], recv_sem=col_recv_sem.at[which, side],
                device_id=to, device_id_type=MESH,
            )
            for side, to in ((0, right), (1, left))
        ]

    def pack_columns(which, block, rows):
        for side, col in ((0, COLS - 1), (1, 0)):
            col_send[which, side, 1 : ROWS + 1] = block[:, col : col + 1, :].astype(F32)
            col_send[which, side, 0:1] = rows[0:1, col : col + 1, :].astype(F32)
            col_send[which, side, ROWS + 1 :] = rows[1:2, col : col + 1, :].astype(F32)

    sends = []
    for which, source, target in ((0, c_hbm, c_rows), (1, x_hbm, x_rows)):
        for copy in row_copies(which, source, target):
            copy.start()
            sends.append(copy)

    def shifted(row):
        wide = row.astype(F32)
        one = jnp.zeros((1, CH), F32)
        return (
            jnp.concatenate([one, wide, one, one], 0).astype(BF16),
            jnp.concatenate([wide, one, one, one], 0).astype(BF16),
            jnp.concatenate([wide[1:], one, one, one, one], 0).astype(BF16),
        )

    def spread(block, target):
        @pl.loop(0, ROWS)
        def _(r):
            for b, value in enumerate(shifted(block[r])):
                target[b, rows_at(r + 1, PITCH), :] = value

        for b in range(3):
            target[b, 0:PITCH, :] = jnp.zeros((PITCH, CH), BF16)
            target[b, (ROWS + 1) * PITCH :, :] = jnp.zeros((FLAT - (ROWS + 1) * PITCH, CH), BF16)

    loads[0].wait()
    spread(c_in, cs)
    loads[1].wait()
    spread(x_in, xs)
    for i in range(DEPTH // 256):
        xt[:, i * 256 : (i + 1) * 256] = xs[1, PITCH + i * 256 : PITCH + (i + 1) * 256, :].T

    row_wait(0, c_rows)
    row_wait(1, x_rows)
    pack_columns(0, c_in, c_rows)
    for copy in col_copies(0):
        copy.start()
        sends.append(copy)
    pack_columns(1, x_in, x_rows)
    for copy in col_copies(1):
        copy.start()
        sends.append(copy)
    loads[2].wait()

    for side in range(2):
        for b, value in enumerate(shifted(c_rows[side])):
            c_halo[b, side] = value
        for b, value in enumerate(shifted(x_rows[side])):
            xs[b, side * (ROWS + 1) * PITCH : side * (ROWS + 1) * PITCH + PITCH, :] = value

    def fill_columns(which, target):
        for side, b, cell in ((0, 0, 0), (1, 2, COLS - 1)):
            @pl.loop(1, ROWS + 1)
            def _(r):
                base = pl.multiple_of(r * PITCH + (cell // 16) * 16, 16)
                block = target[b, pl.ds(base, 16), :].astype(F32)
                at = lax.broadcasted_iota(jnp.int32, (16, CH), 0) == cell % 16
                target[b, pl.ds(base, 16), :] = jnp.where(at, col_recv[which, side, r], block).astype(BF16)

    def fill_row(which, row, side, b, cell):
        at = lax.broadcasted_iota(jnp.int32, (PITCH, CH), 0) == cell
        edge = col_recv[which, side, row]
        return lambda value: jnp.where(at, edge, value.astype(F32)).astype(BF16)

    def tap_of(t):
        return (1 + 2 * (t % 3)) % 3, (1 + 2 * (t // 3)) % 3

    top_tap = jnp.where(north, 0, 2)
    bottom_tap = jnp.where(south, 2, 0)

    def pair_copy(t):
        return pltpu.make_async_remote_copy(
            src_ref=term.at[t, 1 - core], dst_ref=pair_recv.at[t],
            send_sem=ar_send_sem.at[0, t], recv_sem=ar_recv_sem.at[0, t],
            device_id=other, device_id_type=MESH,
        )

    def axes(t):
        odd = t % 2
        first = odd * y + (1 - odd) * xc
        second = odd * xc + (1 - odd) * y
        return odd, first, second

    def first_peer(t, d):
        odd = t % 2
        return device((xc + d * (1 - odd)) % NX, (y + d * odd) % NY, z, core)

    def second_peer(t, d):
        odd = t % 2
        return device((xc + d * odd) % NX, (y + d * (1 - odd)) % NY, z, core)

    def remote(src, dst, phase, t, to):
        pltpu.make_async_remote_copy(
            src_ref=src, dst_ref=dst, send_sem=ar_send_sem.at[phase, t], recv_sem=ar_recv_sem.at[phase, t],
            device_id=to, device_id_type=MESH,
        ).start()

    def arrived(ref, phase, t):
        pltpu.make_async_copy(ref, ref, ar_recv_sem.at[phase, t]).wait()

    def phase1(t):
        arrived(pair_recv.at[t], 0, t)
        half[t] = term[t, core] + pair_recv[t]
        _, first, _ = axes(t)
        for d in range(1, 4):
            remote(half.at[t, (first + d) % 4], recv1.at[t, d - 1], 1, t, first_peer(t, d))

    def phase2(t):
        arrived(recv1.at[t], 1, t)
        _, first, second = axes(t)
        sum1[t] = (half[t, first] + recv1[t, 0]) + (recv1[t, 1] + recv1[t, 2])
        for d in range(1, 4):
            remote(sum1.at[t, (second + d) % 4], recv2.at[t, d - 1], 2, t, second_peer(t, d))

    def phase3(t):
        arrived(recv2.at[t], 2, t)
        _, _, second = axes(t)
        recv3[t, z] = (sum1[t, second] + recv2[t, 0]) + (recv2[t, 1] + recv2[t, 2])
        for d in range(1, 8):
            remote(recv3.at[t, z], recv3.at[t, z], 3, t, device(xc, y, (z + d) % NZ, core))

    def phase4(t):
        arrived(recv3.at[t, 0:7], 3, t)
        _, first, second = axes(t)
        pairs = [recv3[t, 2 * i] + recv3[t, 2 * i + 1] for i in range(4)]
        final[t, core, first, second] = ((pairs[0] + pairs[1]) + (pairs[2] + pairs[3])) * scale
        piece = final.at[t, core, first, second]
        for d in range(1, 4):
            remote(piece, piece, 4, t, second_peer(t, d))

    def phase5(t):
        arrived(recv2.at[t], 4, t)
        _, first, _ = axes(t)
        piece = final.at[t, core, first]
        for d in range(1, 4):
            remote(piece, piece, 5, t, first_peer(t, d))

    def phase6(t):
        arrived(recv1.at[t], 5, t)
        remote(final.at[t, core], final.at[t, core], 6, t, other)

    def kg_copy(t, side):
        a, b = tap_of(t)
        return pltpu.make_async_copy(
            final.at[t, side], kg_hbm.at[a * 3 + b, :, :, :, side * 128 : side * 128 + 128], kg_sem.at[t, side]
        )

    def phase7(t):
        arrived(pair_recv.at[t], 6, t)
        for side in range(2):
            kg_copy(t, side).start()

    phases = [phase1, phase2, phase3, phase4, phase5, phase6, phase7]

    def weight_tap(t):
        a, b = tap_of(t)
        res = jnp.dot(xt[...], cs[2 - b, rows_at(2 - a, DEPTH), :], preferred_element_type=F32)
        term[t, 0] = res[:, :128].reshape(4, 4, 16, 128)
        term[t, 1] = res[:, 128:].reshape(4, 4, 16, 128)
        for side, tap, row in ((0, top_tap, 1), (1, bottom_tap, ROWS)):
            @pl.when(a == tap)
            def _():
                more = lax.dot_general(
                    xs[1, row * PITCH : row * PITCH + PITCH, :], c_halo[2 - b, side],
                    (((0,), (0,)), ((), ())), preferred_element_type=F32,
                )
                term[t, 0] += more[:, :128].reshape(4, 4, 16, 128)
                term[t, 1] += more[:, 128:].reshape(4, 4, 16, 128)
        pair_copy(t).start()

    def out_copy(i, which):
        value, target = ((out_v, out_hbm), (grad_v, grad_hbm))[which]
        part = pl.ds(i * TILE, TILE)
        return pltpu.make_async_copy(value.at[part], target.at[part], store_sem.at[which, i])

    def out_tile(i):
        acc = None
        for a in range(3):
            for b in range(3):
                part = jnp.dot(
                    xs[b, rows_at(i * TILE + a, TILE * PITCH), :], w[a, b], preferred_element_type=F32
                )
                acc = part if acc is None else acc + part
        out_v[pl.ds(i * TILE, TILE)] = acc.astype(BF16).reshape(TILE, PITCH, CH)[:, :COLS]
        out_copy(i, 0).start()

    def times_transposed(rows, weights):
        return lax.dot_general(rows, weights, (((1,), (1,)), ((), ())), preferred_element_type=F32)

    def grad_rows(row, count):
        acc = None
        for a in range(3):
            for b in range(3):
                part = times_transposed(cs[2 - b, rows_at(row + 2 - a, count * PITCH), :], w[a, b])
                acc = part if acc is None else acc + part
        return acc

    def grad_tile(i):
        grad_v[pl.ds(i * TILE, TILE)] = (
            grad_rows(i * TILE, TILE).astype(BF16).reshape(TILE, PITCH, CH)[:, :COLS]
        )
        for side, tile, row, tap in ((0, 0, 0, top_tap), (1, TILES - 1, ROWS - 1, bottom_tap)):
            @pl.when(i == tile)
            def _():
                acc = grad_rows(row, 1)
                for b in range(3):
                    acc = acc + times_transposed(c_halo[2 - b, side], w[tap, b])
                grad_v[row] = acc.astype(BF16)[:COLS]
        out_copy(i, 1).start()

    @pl.loop(0, TAPS + GAP * len(phases))
    def _(s):
        for p in range(len(phases), 0, -1):
            t = s - GAP * p

            @pl.when((t >= 0) & (t < TAPS))
            def _():
                phases[p - 1](t)

        @pl.when(s == 3)
        def _():
            for side in range(2):
                pltpu.make_async_copy(
                    col_recv.at[0, side], col_recv.at[0, side], col_recv_sem.at[0, side]
                ).wait()
            fill_columns(0, cs)
            for side, b, cell in ((0, 0, 0), (1, 2, COLS - 1)):
                for end in range(2):
                    put = fill_row(0, end * (ROWS + 1), side, b, cell)
                    c_halo[b, end] = put(c_halo[b, end])

        @pl.when(s < TAPS)
        def _():
            weight_tap(s)

        @pl.when(s == TAPS)
        def _():
            for side in range(2):
                pltpu.make_async_copy(
                    col_recv.at[1, side], col_recv.at[1, side], col_recv_sem.at[1, side]
                ).wait()
            fill_columns(1, xs)
            for side, b, cell in ((0, 0, 0), (1, 2, COLS - 1)):
                for end in range(2):
                    put = fill_row(1, end * (ROWS + 1), side, b, cell)
                    place = slice(end * (ROWS + 1) * PITCH, end * (ROWS + 1) * PITCH + PITCH)
                    xs[b, place, :] = put(xs[b, place, :])

        @pl.when((s >= TAPS) & (s < TAPS + TILES))
        def _():
            out_tile(s - TAPS)

        @pl.when((s >= TAPS + TILES) & (s < STEPS))
        def _():
            grad_tile(s - TAPS - TILES)

    for copy in sends:
        copy.wait_send()

    @pl.loop(0, TAPS)
    def _(t):
        for phase, ref in enumerate((pair_recv, recv1, recv2, recv3.at[:, 0:7], recv2, recv1, pair_recv)):
            pltpu.make_async_copy(ref.at[t], ref.at[t], ar_send_sem.at[phase, t]).wait()
        for side in range(2):
            kg_copy(t, side).wait()

    @pl.loop(0, TILES)
    def _(i):
        for which in range(2):
            out_copy(i, which).wait()


def local(inputs, weights, cotangent):
    scale = 1.0 / math.sqrt(ROWS * COLS * lax.axis_size("lat") * lax.axis_size("lon"))
    block = jax.ShapeDtypeStruct((ROWS, COLS, CH), BF16)
    anywhere = pl.BlockSpec(memory_space=pl.ANY)
    dma = pltpu.SemaphoreType.DMA
    outputs, grad, kg = pl.pallas_call(
        functools.partial(kernel, scale),
        out_shape=(block, block, jax.ShapeDtypeStruct((TAPS, 4, 4, 16, CH), F32)),
        in_specs=[anywhere] * 3,
        out_specs=(anywhere,) * 3,
        scratch_shapes=[
            pltpu.VMEM((ROWS, COLS, CH), BF16),
            pltpu.VMEM((ROWS, COLS, CH), BF16),
            pltpu.VMEM((3, 3, CH, CH), BF16),
            pltpu.VMEM((3, FLAT, CH), BF16),
            pltpu.VMEM((3, FLAT, CH), BF16),
            pltpu.VMEM((CH, DEPTH), BF16),
            pltpu.VMEM((2, COLS, CH), BF16),
            pltpu.VMEM((2, COLS, CH), BF16),
            pltpu.VMEM((3, 2, PITCH, CH), BF16),
            pltpu.VMEM((2, 2, ROWS + 2, 1, CH), F32),
            pltpu.VMEM((2, 2, ROWS + 2, 1, CH), F32),
            pltpu.VMEM((ROWS, COLS, CH), BF16),
            pltpu.VMEM((ROWS, COLS, CH), BF16),
            pltpu.VMEM((TAPS, 2, 4, 4, 16, 128), F32),
            pltpu.VMEM((TAPS, 4, 4, 16, 128), F32),
            pltpu.VMEM((TAPS, 4, 4, 16, 128), F32),
            pltpu.VMEM((TAPS, 3, 4, 16, 128), F32),
            pltpu.VMEM((TAPS, 4, 16, 128), F32),
            pltpu.VMEM((TAPS, 3, 16, 128), F32),
            pltpu.VMEM((TAPS, 8, 16, 128), F32),
            pltpu.VMEM((TAPS, 2, 4, 4, 16, 128), F32),
            dma((3,)),
            dma((2, TILES)),
            dma((TAPS, 2)),
            dma((2, 2)),
            dma((2, 2)),
            dma((2, 2)),
            dma((2, 2)),
            dma((7, TAPS)),
            dma((7, TAPS)),
        ],
        compiler_params=pltpu.CompilerParams(
            collective_id=0, has_side_effects=True, vmem_limit_bytes=56 * 2**20
        ),
        cost_estimate=pl.CostEstimate(flops=15 * 10**9, bytes_accessed=12 * 10**6, transcendentals=0),
    )(inputs, weights, cotangent)
    return outputs, grad, kg.reshape(3, 3, CH, CH)


def solution(mesh):
    in_specs = (P("lat", "lon", None), P(), P("lat", "lon", None))
    out_specs = (P("lat", "lon", None), P("lat", "lon", None), P())
    return jax.shard_map(local, mesh=mesh, in_specs=in_specs, out_specs=out_specs, check_vma=False)
```

```python
import functools
import math

import jax
import jax.numpy as jnp
from jax import lax
from jax.experimental import pallas as pl
from jax.experimental.pallas import tpu as pltpu
from jax.sharding import PartitionSpec as P

MESH = pl.DeviceIdType.MESH
F32 = jnp.float32
BF16 = jnp.bfloat16

ROWS, COLS, CH = 90, 45, 256
PITCH = 48
FLAT = (ROWS + 2) * PITCH + 32
DEPTH = 4352
NX, NY, NZ = 4, 4, 8
TILE = 10
TILES = ROWS // TILE
TAPS = 9
WAITS = (2, 7, 12, 17, 19)
STEPS = TAPS + 2 * TILES


def rows_at(row, count):
    return pl.ds(pl.multiple_of(row * PITCH, 16), count)


def kernel(
    scale,
    x_hbm, w_hbm, c_hbm,
    out_v, grad_v, kg_v,
    x_in, c_in, w,
    xs, cs, xt, x_rows, c_rows, c_halo,
    col_send, col_recv, corner_send, corner_recv,
    term, pair_recv, half, plane_recv, line, final,
    load_sem,
    row_send_sem, row_recv_sem, col_send_sem, col_recv_sem, corner_send_sem, corner_recv_sem,
    ar_send_sem, ar_recv_sem,
):
    lat, lon = lax.axis_index("lat"), lax.axis_index("lon")
    x_hi, y = lat // 4, lat % 4
    x_lo, z, core = lon // 16, (lon // 2) % 8, lon % 2
    xc = x_hi * 2 + x_lo

    def device(xx, yy, zz, cc):
        return ((xx // 2) * 4 + yy, ((xx % 2) * 8 + zz) * 2 + cc)

    north, south = lat == 0, lat == 7
    across = (lon + 16) % 32
    up = (jnp.where(north, 0, lat - 1), jnp.where(north, across, lon))
    down = (jnp.where(south, 7, lat + 1), jnp.where(south, across, lon))
    left, right = (lat, (lon + 31) % 32), (lat, (lon + 1) % 32)
    other = device(xc, y, z, 1 - core)

    def plane_peer(d):
        return device((xc + d // 4) % NX, (y + d % 4) % NY, z, core)

    loads = [
        pltpu.make_async_copy(c_hbm, c_in, load_sem.at[0]),
        pltpu.make_async_copy(x_hbm, x_in, load_sem.at[1]),
        pltpu.make_async_copy(w_hbm, w, load_sem.at[2]),
    ]
    for load in loads:
        load.start()

    barrier = pltpu.get_barrier_semaphore()
    friends = [device(xc, y, (z + d) % NZ, core) for d in (4, 3, 5, 2, 6, 1, 7)]
    friends += [plane_peer(d) for d in range(1, 16)]
    friends += [up, down, left, right, other]
    for friend in friends:
        pl.semaphore_signal(barrier, inc=1, device_id=friend, device_id_type=MESH)
    pl.semaphore_wait(barrier, len(friends))

    def row_copies(which, source, target):
        to_up, to_down = jnp.where(north, 0, 1), jnp.where(south, 1, 0)
        return [
            pltpu.make_async_remote_copy(
                src_ref=source.at[0], dst_ref=target.at[to_up],
                send_sem=row_send_sem.at[which, 0], recv_sem=row_recv_sem.at[which, to_up],
                device_id=up, device_id_type=MESH,
            ),
            pltpu.make_async_remote_copy(
                src_ref=source.at[ROWS - 1], dst_ref=target.at[to_down],
                send_sem=row_send_sem.at[which, 1], recv_sem=row_recv_sem.at[which, to_down],
                device_id=down, device_id_type=MESH,
            ),
        ]

    def row_wait(which, target):
        for side in range(2):
            pltpu.make_async_copy(target.at[side], target.at[side], row_recv_sem.at[which, side]).wait()

    def col_copies(which):
        return [
            pltpu.make_async_remote_copy(
                src_ref=col_send.at[which, side], dst_ref=col_recv.at[which, side],
                send_sem=col_send_sem.at[which, side], recv_sem=col_recv_sem.at[which, side],
                device_id=to, device_id_type=MESH,
            )
            for side, to in ((0, right), (1, left))
        ]

    def corner_copies(which):
        return [
            pltpu.make_async_remote_copy(
                src_ref=corner_send.at[which, side], dst_ref=corner_recv.at[which, side],
                send_sem=corner_send_sem.at[which, side], recv_sem=corner_recv_sem.at[which, side],
                device_id=to, device_id_type=MESH,
            )
            for side, to in ((0, right), (1, left))
        ]

    def send_columns(which, block):
        for side, col in ((0, COLS - 1), (1, 0)):
            col_send[which, side] = block[:, col : col + 1, :].astype(F32)
            col_copies(which)[side].start()

    def send_corners(which, rows):
        for side, col in ((0, COLS - 1), (1, 0)):
            corner_send[which, side] = rows[:, col : col + 1, :].astype(F32)
            corner_copies(which)[side].start()

    def wait_corners(which):
        for side in range(2):
            pltpu.make_async_copy(
                corner_recv.at[which, side], corner_recv.at[which, side], corner_recv_sem.at[which, side]
            ).wait()

    def centred(row):
        return jnp.concatenate([row, jnp.zeros((PITCH - COLS, CH), BF16)], 0)

    def sideways(row, before, after):
        wide = row.astype(F32)
        pad = jnp.zeros((PITCH - COLS, CH), F32)
        return (
            (0, jnp.concatenate([before, wide, pad[1:]], 0).astype(BF16)),
            (2, jnp.concatenate([wide[1:], after, pad], 0).astype(BF16)),
        )

    def spread_centre(block, target):
        @pl.loop(0, ROWS, unroll=5)
        def _(r):
            target[1, rows_at(r + 1, PITCH), :] = centred(block[r])

        for b in range(3):
            target[b, 0:PITCH, :] = jnp.zeros((PITCH, CH), BF16)
            target[b, (ROWS + 1) * PITCH :, :] = jnp.zeros((FLAT - (ROWS + 1) * PITCH, CH), BF16)

    def spread_sides(which, block, target):
        for side in range(2):
            pltpu.make_async_copy(
                col_recv.at[which, side], col_recv.at[which, side], col_recv_sem.at[which, side]
            ).wait()

        @pl.loop(0, ROWS, unroll=5)
        def _(r):
            for b, value in sideways(block[r], col_recv[which, 0, r], col_recv[which, 1, r]):
                target[b, rows_at(r + 1, PITCH), :] = value

    def send_rows(which, block, rows):
        for copy in row_copies(which, block, rows):
            copy.start()

    loads[0].wait()
    send_rows(0, c_in, c_rows)
    send_columns(0, c_in)
    spread_centre(c_in, cs)
    loads[1].wait()
    spread_centre(x_in, xs)
    for i in range(DEPTH // 256):
        xt[:, i * 256 : (i + 1) * 256] = xs[1, PITCH + i * 256 : PITCH + (i + 1) * 256, :].T
    row_wait(0, c_rows)
    send_corners(0, c_rows)
    for end in range(2):
        c_halo[1, end] = centred(c_rows[end])
    send_rows(1, x_in, x_rows)
    send_columns(1, x_in)

    def tap_of(t):
        late = t - 5
        a_early = jnp.where(t == 1, 0, jnp.where(t == 2, 2, 1))
        b_early = jnp.where(t == 3, 0, jnp.where(t == 4, 2, 1))
        corner = t >= 5
        return (
            jnp.where(corner, (late // 2) * 2, a_early),
            jnp.where(corner, (late % 2) * 2, b_early),
        )

    top_tap = jnp.where(north, 0, 2)
    bottom_tap = jnp.where(south, 2, 0)

    def pair_copy(t):
        return pltpu.make_async_remote_copy(
            src_ref=term.at[t, 1 - core], dst_ref=pair_recv.at[t],
            send_sem=ar_send_sem.at[0, t], recv_sem=ar_recv_sem.at[0, t],
            device_id=other, device_id_type=MESH,
        )

    def remote(src, dst, phase, t, to):
        pltpu.make_async_remote_copy(
            src_ref=src, dst_ref=dst, send_sem=ar_send_sem.at[phase, t], recv_sem=ar_recv_sem.at[phase, t],
            device_id=to, device_id_type=MESH,
        ).start()

    def arrived(ref, phase, t):
        pltpu.make_async_copy(ref, ref, ar_recv_sem.at[phase, t]).wait()

    def to_plane(t):
        arrived(pair_recv.at[t], 0, t)
        half[t] = term[t, core] + pair_recv[t]
        for d in range(1, 16):
            piece = half.at[t, (xc + d // 4) % NX, (y + d % 4) % NY]
            remote(piece, plane_recv.at[t, d - 1], 1, t, plane_peer(d))

    def to_line(t):
        arrived(plane_recv.at[t], 1, t)
        parts = [half[t, xc, y]] + [plane_recv[t, d] for d in range(15)]
        while len(parts) > 1:
            parts = [parts[i] + parts[i + 1] for i in range(0, len(parts), 2)]
        line[t, z] = parts[0]
        for d in (4, 3, 5, 2, 6, 1, 7):
            remote(line.at[t, z], line.at[t, z], 2, t, device(xc, y, (z + d) % NZ, core))

    def from_line(t):
        arrived(line.at[t, 0:7], 2, t)
        parts = [line[t, i] for i in range(NZ)]
        while len(parts) > 1:
            parts = [parts[i] + parts[i + 1] for i in range(0, len(parts), 2)]
        final[t, core, xc, y] = parts[0] * scale
        piece = final.at[t, core, xc, y]
        for d in range(1, 16):
            remote(piece, piece, 3, t, plane_peer(d))

    def to_pair(t):
        arrived(plane_recv.at[t], 3, t)
        remote(final.at[t, core], final.at[t, core], 4, t, other)

    def finish(t):
        arrived(pair_recv.at[t], 4, t)
        a, b = tap_of(t)
        kg_v[a * 3 + b, :, :, :, :128] = final[t, 0]
        kg_v[a * 3 + b, :, :, :, 128:] = final[t, 1]

    plan = list(zip(WAITS, (to_plane, to_line, from_line, to_pair, finish)))

    def communicate(s, begin, end):
        for wait, phase in reversed(plan):
            if wait < end and TAPS + wait > begin:
                t = s - wait

                @pl.when((t >= 0) & (t < TAPS))
                def _():
                    phase(t)

    def weight_tap(t):
        a, b = tap_of(t)
        res = jnp.dot(xt[...], cs[2 - b, rows_at(2 - a, DEPTH), :], preferred_element_type=F32)
        term[t, 0] = res[:, :128].reshape(4, 4, 16, 128)
        term[t, 1] = res[:, 128:].reshape(4, 4, 16, 128)
        for side, tap, row in ((0, top_tap, 1), (1, bottom_tap, ROWS)):
            @pl.when(a == tap)
            def _():
                more = lax.dot_general(
                    xs[1, row * PITCH : row * PITCH + PITCH, :], c_halo[2 - b, side],
                    (((0,), (0,)), ((), ())), preferred_element_type=F32,
                )
                term[t, 0] += more[:, :128].reshape(4, 4, 16, 128)
                term[t, 1] += more[:, 128:].reshape(4, 4, 16, 128)
        pair_copy(t).start()

    def out_tile(i):
        acc = None
        for a in range(3):
            for b in range(3):
                part = jnp.dot(
                    xs[b, rows_at(i * TILE + a, TILE * PITCH), :], w[a, b], preferred_element_type=F32
                )
                acc = part if acc is None else acc + part
        out_v[pl.ds(i * TILE, TILE)] = acc.astype(BF16).reshape(TILE, PITCH, CH)[:, :COLS]

    def times_transposed(rows, weights):
        return lax.dot_general(rows, weights, (((1,), (1,)), ((), ())), preferred_element_type=F32)

    def grad_rows(row, count):
        acc = None
        for a in range(3):
            for b in range(3):
                part = times_transposed(cs[2 - b, rows_at(row + 2 - a, count * PITCH), :], w[a, b])
                acc = part if acc is None else acc + part
        return acc

    def grad_tile(i):
        grad_v[pl.ds(i * TILE, TILE)] = (
            grad_rows(i * TILE, TILE).astype(BF16).reshape(TILE, PITCH, CH)[:, :COLS]
        )
        for side, tile, row, tap in ((0, 0, 0, top_tap), (1, TILES - 1, ROWS - 1, bottom_tap)):
            @pl.when(i == tile)
            def _():
                acc = grad_rows(row, 1)
                for b in range(3):
                    acc = acc + times_transposed(c_halo[2 - b, side], w[tap, b])
                grad_v[row] = acc.astype(BF16)[:COLS]

    def edge_rows(which, rows):
        for end in range(2):
            for b, value in sideways(rows[end], corner_recv[which, 0, end], corner_recv[which, 1, end]):
                yield end, b, value

    @pl.loop(0, TAPS)
    def _(s):
        communicate(s, 0, TAPS)

        @pl.when(s == 2)
        def _():
            row_wait(1, x_rows)
            send_corners(1, x_rows)
            for end in range(2):
                place = slice(end * (ROWS + 1) * PITCH, end * (ROWS + 1) * PITCH + PITCH)
                xs[1, place, :] = centred(x_rows[end])

        @pl.when(s == 3)
        def _():
            spread_sides(0, c_in, cs)

        @pl.when(s == 5)
        def _():
            wait_corners(0)
            for end, b, value in edge_rows(0, c_rows):
                c_halo[b, end] = value

        weight_tap(s)

    loads[2].wait()
    spread_sides(1, x_in, xs)
    wait_corners(1)
    for end, b, value in edge_rows(1, x_rows):
        xs[b, end * (ROWS + 1) * PITCH : end * (ROWS + 1) * PITCH + PITCH, :] = value

    @pl.loop(TAPS, TAPS + TILES)
    def _(s):
        communicate(s, TAPS, TAPS + TILES)
        out_tile(s - TAPS)

    @pl.loop(TAPS + TILES, STEPS)
    def _(s):
        communicate(s, TAPS + TILES, STEPS)
        grad_tile(s - TAPS - TILES)

    last = TAPS + WAITS[-1]

    @pl.loop(STEPS, last)
    def _(s):
        communicate(s, STEPS, last)

    for which, block, rows in ((0, c_in, c_rows), (1, x_in, x_rows)):
        for copy in row_copies(which, block, rows) + col_copies(which) + corner_copies(which):
            copy.wait_send()

    def sent(ref, phase, t):
        pltpu.make_async_copy(ref, ref, ar_send_sem.at[phase, t]).wait()

    @pl.loop(0, TAPS)
    def _(t):
        for phase, ref in enumerate(
            (pair_recv.at[t], plane_recv.at[t], line.at[t, 0:7], plane_recv.at[t], pair_recv.at[t])
        ):
            sent(ref, phase, t)


def store_kernel(*refs):
    sems = refs[6]
    copies = [pltpu.make_async_copy(refs[i], refs[i + 3], sems.at[i]) for i in range(3)]
    for copy in copies:
        copy.start()
    for copy in copies:
        copy.wait()


def local(inputs, weights, cotangent):
    scale = 1.0 / math.sqrt(ROWS * COLS * lax.axis_size("lat") * lax.axis_size("lon"))
    block = pltpu.VMEM((ROWS, COLS, CH), BF16)
    anywhere = pl.BlockSpec(memory_space=pl.ANY)
    dma = pltpu.SemaphoreType.DMA
    outputs, grad, kg = pl.pallas_call(
        functools.partial(kernel, scale),
        out_shape=(block, block, pltpu.VMEM((TAPS, 4, 4, 16, CH), F32)),
        in_specs=[anywhere] * 3,
        out_specs=(pl.BlockSpec(memory_space=pltpu.VMEM),) * 3,
        scratch_shapes=[
            pltpu.VMEM((ROWS, COLS, CH), BF16),
            pltpu.VMEM((ROWS, COLS, CH), BF16),
            pltpu.VMEM((3, 3, CH, CH), BF16),
            pltpu.VMEM((3, FLAT, CH), BF16),
            pltpu.VMEM((3, FLAT, CH), BF16),
            pltpu.VMEM((CH, DEPTH), BF16),
            pltpu.VMEM((2, COLS, CH), BF16),
            pltpu.VMEM((2, COLS, CH), BF16),
            pltpu.VMEM((3, 2, PITCH, CH), BF16),
            pltpu.VMEM((2, 2, ROWS, 1, CH), F32),
            pltpu.VMEM((2, 2, ROWS, 1, CH), F32),
            pltpu.VMEM((2, 2, 2, 1, CH), F32),
            pltpu.VMEM((2, 2, 2, 1, CH), F32),
            pltpu.VMEM((TAPS, 2, 4, 4, 16, 128), F32),
            pltpu.VMEM((TAPS, 4, 4, 16, 128), F32),
            pltpu.VMEM((TAPS, 4, 4, 16, 128), F32),
            pltpu.VMEM((TAPS, 15, 16, 128), F32),
            pltpu.VMEM((TAPS, NZ, 16, 128), F32),
            pltpu.VMEM((TAPS, 2, 4, 4, 16, 128), F32),
            dma((3,)),
            dma((2, 2)),
            dma((2, 2)),
            dma((2, 2)),
            dma((2, 2)),
            dma((2, 2)),
            dma((2, 2)),
            dma((5, TAPS)),
            dma((5, TAPS)),
        ],
        compiler_params=pltpu.CompilerParams(
            collective_id=0, has_side_effects=True, vmem_limit_bytes=56 * 2**20
        ),
        cost_estimate=pl.CostEstimate(flops=15 * 10**9, bytes_accessed=12 * 10**6, transcendentals=0),
    )(inputs, weights, cotangent)
    outputs, grad, kg = pl.pallas_call(
        store_kernel,
        out_shape=tuple(jax.ShapeDtypeStruct(v.shape, v.dtype) for v in (outputs, grad, kg)),
        in_specs=[anywhere] * 3,
        out_specs=(anywhere,) * 3,
        scratch_shapes=[dma((3,))],
        compiler_params=pltpu.CompilerParams(vmem_limit_bytes=2**20),
    )(outputs, grad, kg)
    return outputs, grad, kg.reshape(3, 3, CH, CH)


def solution(mesh):
    in_specs = (P("lat", "lon", None), P(), P("lat", "lon", None))
    out_specs = (P("lat", "lon", None), P("lat", "lon", None), P())
    return jax.shard_map(local, mesh=mesh, in_specs=in_specs, out_specs=out_specs, check_vma=False)
```

```python
import functools
import math

import jax
import jax.numpy as jnp
from jax import lax
from jax.experimental import pallas as pl
from jax.experimental.pallas import tpu as pltpu
from jax.sharding import PartitionSpec as P

MESH = pl.DeviceIdType.MESH
F32 = jnp.float32
BF16 = jnp.bfloat16

ROWS, COLS, CH = 90, 45, 256
PITCH = 48
FLAT = (ROWS + 2) * PITCH + 32
DEPTH = 4352
NX, NY, NZ = 4, 4, 8
TILE = 15
TILES = ROWS // TILE
TAPS = 9
WAITS = (2, 7, 11, 15, 17)
PLANE_ORDER = (10, 5, 15, 7, 13, 2, 8, 6, 9, 14, 11, 1, 4, 3, 12)
STEPS = TAPS + 2 * TILES


def rows_at(row, count):
    return pl.ds(pl.multiple_of(row * PITCH, 16), count)


def kernel(
    scale,
    x_hbm, w_hbm, c_hbm,
    out_v, grad_v, kg_v,
    x_in, c_in, w,
    xs, cs, xt, x_rows, c_rows, c_halo,
    col_send, col_recv, corner_send, corner_recv,
    term, pair_recv, half, plane_recv, line, final,
    load_sem,
    row_send_sem, row_recv_sem, col_send_sem, col_recv_sem, corner_send_sem, corner_recv_sem,
    ar_send_sem, ar_recv_sem,
):
    lat, lon = lax.axis_index("lat"), lax.axis_index("lon")
    x_hi, y = lat // 4, lat % 4
    x_lo, z, core = lon // 16, (lon // 2) % 8, lon % 2
    xc = x_hi * 2 + x_lo

    def device(xx, yy, zz, cc):
        return ((xx // 2) * 4 + yy, ((xx % 2) * 8 + zz) * 2 + cc)

    north, south = lat == 0, lat == 7
    across = (lon + 16) % 32
    up = (jnp.where(north, 0, lat - 1), jnp.where(north, across, lon))
    down = (jnp.where(south, 7, lat + 1), jnp.where(south, across, lon))
    left, right = (lat, (lon + 31) % 32), (lat, (lon + 1) % 32)
    other = device(xc, y, z, 1 - core)

    def plane_peer(d):
        return device((xc + d // 4) % NX, (y + d % 4) % NY, z, core)

    loads = [
        pltpu.make_async_copy(c_hbm, c_in, load_sem.at[0]),
        pltpu.make_async_copy(x_hbm, x_in, load_sem.at[1]),
        pltpu.make_async_copy(w_hbm, w, load_sem.at[2]),
    ]
    for load in loads:
        load.start()

    barrier = pltpu.get_barrier_semaphore()
    friends = [device(xc, y, (z + d) % NZ, core) for d in (4, 3, 5, 2, 6, 1, 7)]
    friends += [plane_peer(d) for d in range(1, 16)]
    friends += [up, down, left, right, other]
    for friend in friends:
        pl.semaphore_signal(barrier, inc=1, device_id=friend, device_id_type=MESH)
    pl.semaphore_wait(barrier, len(friends))

    def row_copies(which, source, target):
        to_up, to_down = jnp.where(north, 0, 1), jnp.where(south, 1, 0)
        return [
            pltpu.make_async_remote_copy(
                src_ref=source.at[0], dst_ref=target.at[to_up],
                send_sem=row_send_sem.at[which, 0], recv_sem=row_recv_sem.at[which, to_up],
                device_id=up, device_id_type=MESH,
            ),
            pltpu.make_async_remote_copy(
                src_ref=source.at[ROWS - 1], dst_ref=target.at[to_down],
                send_sem=row_send_sem.at[which, 1], recv_sem=row_recv_sem.at[which, to_down],
                device_id=down, device_id_type=MESH,
            ),
        ]

    def row_wait(which, target):
        for side in range(2):
            pltpu.make_async_copy(target.at[side], target.at[side], row_recv_sem.at[which, side]).wait()

    def col_copies(which):
        return [
            pltpu.make_async_remote_copy(
                src_ref=col_send.at[which, side], dst_ref=col_recv.at[which, side],
                send_sem=col_send_sem.at[which, side], recv_sem=col_recv_sem.at[which, side],
                device_id=to, device_id_type=MESH,
            )
            for side, to in ((0, right), (1, left))
        ]

    def corner_copies(which):
        return [
            pltpu.make_async_remote_copy(
                src_ref=corner_send.at[which, side], dst_ref=corner_recv.at[which, side],
                send_sem=corner_send_sem.at[which, side], recv_sem=corner_recv_sem.at[which, side],
                device_id=to, device_id_type=MESH,
            )
            for side, to in ((0, right), (1, left))
        ]

    def send_columns(which, block):
        for side, col in ((0, COLS - 1), (1, 0)):
            col_send[which, side] = block[:, col : col + 1, :].astype(F32)
            col_copies(which)[side].start()

    def send_corners(which, rows):
        for side, col in ((0, COLS - 1), (1, 0)):
            corner_send[which, side] = rows[:, col : col + 1, :].astype(F32)
            corner_copies(which)[side].start()

    def wait_corners(which):
        for side in range(2):
            pltpu.make_async_copy(
                corner_recv.at[which, side], corner_recv.at[which, side], corner_recv_sem.at[which, side]
            ).wait()

    def centred(row):
        return jnp.concatenate([row, jnp.zeros((PITCH - COLS, CH), BF16)], 0)

    def sideways(row, before, after):
        wide = row.astype(F32)
        pad = jnp.zeros((PITCH - COLS, CH), F32)
        return (
            (0, jnp.concatenate([before, wide, pad[1:]], 0).astype(BF16)),
            (2, jnp.concatenate([wide[1:], after, pad], 0).astype(BF16)),
        )

    def spread_centre(block, target):
        @pl.loop(0, ROWS, unroll=5)
        def _(r):
            target[1, rows_at(r + 1, PITCH), :] = centred(block[r])

        for b in range(3):
            target[b, 0:PITCH, :] = jnp.zeros((PITCH, CH), BF16)
            target[b, (ROWS + 1) * PITCH :, :] = jnp.zeros((FLAT - (ROWS + 1) * PITCH, CH), BF16)

    def spread_sides(which, block, target):
        for side in range(2):
            pltpu.make_async_copy(
                col_recv.at[which, side], col_recv.at[which, side], col_recv_sem.at[which, side]
            ).wait()

        @pl.loop(0, ROWS, unroll=5)
        def _(r):
            for b, value in sideways(block[r], col_recv[which, 0, r], col_recv[which, 1, r]):
                target[b, rows_at(r + 1, PITCH), :] = value

    def send_rows(which, block, rows):
        for copy in row_copies(which, block, rows):
            copy.start()

    loads[0].wait()
    send_rows(0, c_in, c_rows)
    send_columns(0, c_in)
    spread_centre(c_in, cs)
    loads[1].wait()
    spread_centre(x_in, xs)
    for i in range(DEPTH // 256):
        xt[:, i * 256 : (i + 1) * 256] = xs[1, PITCH + i * 256 : PITCH + (i + 1) * 256, :].T

    def tap_of(t):
        late = t - 5
        a_early = jnp.where(t == 1, 0, jnp.where(t == 2, 2, 1))
        b_early = jnp.where(t == 3, 0, jnp.where(t == 4, 2, 1))
        corner = t >= 5
        return (
            jnp.where(corner, (late // 2) * 2, a_early),
            jnp.where(corner, (late % 2) * 2, b_early),
        )

    top_tap = jnp.where(north, 0, 2)
    bottom_tap = jnp.where(south, 2, 0)

    def pair_copy(t):
        return pltpu.make_async_remote_copy(
            src_ref=term.at[t, 1 - core], dst_ref=pair_recv.at[t],
            send_sem=ar_send_sem.at[0, t], recv_sem=ar_recv_sem.at[0, t],
            device_id=other, device_id_type=MESH,
        )

    def remote(src, dst, phase, t, to):
        pltpu.make_async_remote_copy(
            src_ref=src, dst_ref=dst, send_sem=ar_send_sem.at[phase, t], recv_sem=ar_recv_sem.at[phase, t],
            device_id=to, device_id_type=MESH,
        ).start()

    def arrived(ref, phase, t):
        pltpu.make_async_copy(ref, ref, ar_recv_sem.at[phase, t]).wait()

    def to_plane(t):
        arrived(pair_recv.at[t], 0, t)
        half[t] = term[t, core] + pair_recv[t]
        for d in PLANE_ORDER:
            piece = half.at[t, (xc + d // 4) % NX, (y + d % 4) % NY]
            remote(piece, plane_recv.at[t, d - 1], 1, t, plane_peer(d))

    def to_line(t):
        arrived(plane_recv.at[t], 1, t)
        parts = [half[t, xc, y]] + [plane_recv[t, d] for d in range(15)]
        while len(parts) > 1:
            parts = [parts[i] + parts[i + 1] for i in range(0, len(parts), 2)]
        line[t, z] = parts[0]
        for d in (4, 3, 5, 2, 6, 1, 7):
            remote(line.at[t, z], line.at[t, z], 2, t, device(xc, y, (z + d) % NZ, core))

    def from_line(t):
        arrived(line.at[t, 0:7], 2, t)
        parts = [line[t, i] for i in range(NZ)]
        while len(parts) > 1:
            parts = [parts[i] + parts[i + 1] for i in range(0, len(parts), 2)]
        final[t, core, xc, y] = parts[0] * scale
        piece = final.at[t, core, xc, y]
        for d in PLANE_ORDER:
            remote(piece, piece, 3, t, plane_peer(d))

    def to_pair(t):
        arrived(plane_recv.at[t], 3, t)
        remote(final.at[t, core], final.at[t, core], 4, t, other)

    def finish(t):
        arrived(pair_recv.at[t], 4, t)
        a, b = tap_of(t)
        kg_v[a * 3 + b, :, :, :, :128] = final[t, 0]
        kg_v[a * 3 + b, :, :, :, 128:] = final[t, 1]

    plan = list(zip(WAITS, (to_plane, to_line, from_line, to_pair, finish)))

    def communicate(s, begin, end):
        for wait, phase in reversed(plan):
            if wait < end and TAPS + wait > begin:
                t = s - wait

                @pl.when((t >= 0) & (t < TAPS))
                def _():
                    phase(t)

    def weight_tap(t):
        a, b = tap_of(t)
        res = jnp.dot(xt[...], cs[2 - b, rows_at(2 - a, DEPTH), :], preferred_element_type=F32)
        term[t, 0] = res[:, :128].reshape(4, 4, 16, 128)
        term[t, 1] = res[:, 128:].reshape(4, 4, 16, 128)
        for side, tap, row in ((0, top_tap, 1), (1, bottom_tap, ROWS)):
            @pl.when(a == tap)
            def _():
                more = lax.dot_general(
                    xs[1, row * PITCH : row * PITCH + PITCH, :], c_halo[2 - b, side],
                    (((0,), (0,)), ((), ())), preferred_element_type=F32,
                )
                term[t, 0] += more[:, :128].reshape(4, 4, 16, 128)
                term[t, 1] += more[:, 128:].reshape(4, 4, 16, 128)
        pair_copy(t).start()

    def out_tile(i):
        acc = None
        for a in range(3):
            for b in range(3):
                part = jnp.dot(
                    xs[b, rows_at(i * TILE + a, TILE * PITCH), :], w[a, b], preferred_element_type=F32
                )
                acc = part if acc is None else acc + part
        out_v[pl.ds(i * TILE, TILE)] = acc.astype(BF16).reshape(TILE, PITCH, CH)[:, :COLS]

    def times_transposed(rows, weights):
        return lax.dot_general(rows, weights, (((1,), (1,)), ((), ())), preferred_element_type=F32)

    def grad_rows(row, count):
        acc = None
        for a in range(3):
            for b in range(3):
                part = times_transposed(cs[2 - b, rows_at(row + 2 - a, count * PITCH), :], w[a, b])
                acc = part if acc is None else acc + part
        return acc

    def grad_tile(i):
        grad_v[pl.ds(i * TILE, TILE)] = (
            grad_rows(i * TILE, TILE).astype(BF16).reshape(TILE, PITCH, CH)[:, :COLS]
        )
        for side, tile, row, tap in ((0, 0, 0, top_tap), (1, TILES - 1, ROWS - 1, bottom_tap)):
            @pl.when(i == tile)
            def _():
                acc = grad_rows(row, 1)
                for b in range(3):
                    acc = acc + times_transposed(c_halo[2 - b, side], w[tap, b])
                grad_v[row] = acc.astype(BF16)[:COLS]

    def edge_rows(which, rows):
        for end in range(2):
            for b, value in sideways(rows[end], corner_recv[which, 0, end], corner_recv[which, 1, end]):
                yield end, b, value

    @pl.loop(0, TAPS)
    def _(s):
        communicate(s, 0, TAPS)

        @pl.when(s == 1)
        def _():
            row_wait(0, c_rows)
            send_corners(0, c_rows)
            for end in range(2):
                c_halo[1, end] = centred(c_rows[end])
            send_rows(1, x_in, x_rows)

        @pl.when(s == 2)
        def _():
            send_columns(1, x_in)

        @pl.when(s == 6)
        def _():
            row_wait(1, x_rows)
            send_corners(1, x_rows)
            for end in range(2):
                place = slice(end * (ROWS + 1) * PITCH, end * (ROWS + 1) * PITCH + PITCH)
                xs[1, place, :] = centred(x_rows[end])

        @pl.when(s == 3)
        def _():
            spread_sides(0, c_in, cs)

        @pl.when(s == 5)
        def _():
            wait_corners(0)
            for end, b, value in edge_rows(0, c_rows):
                c_halo[b, end] = value

        weight_tap(s)

    loads[2].wait()
    spread_sides(1, x_in, xs)
    wait_corners(1)
    for end, b, value in edge_rows(1, x_rows):
        xs[b, end * (ROWS + 1) * PITCH : end * (ROWS + 1) * PITCH + PITCH, :] = value

    @pl.loop(TAPS, TAPS + TILES)
    def _(s):
        communicate(s, TAPS, TAPS + TILES)
        out_tile(s - TAPS)

    @pl.loop(TAPS + TILES, STEPS)
    def _(s):
        communicate(s, TAPS + TILES, STEPS)
        grad_tile(s - TAPS - TILES)

    last = TAPS + WAITS[-1]

    @pl.loop(STEPS, last)
    def _(s):
        communicate(s, STEPS, last)

    for which, block, rows in ((0, c_in, c_rows), (1, x_in, x_rows)):
        for copy in row_copies(which, block, rows) + col_copies(which) + corner_copies(which):
            copy.wait_send()

    def sent(ref, phase, t):
        pltpu.make_async_copy(ref, ref, ar_send_sem.at[phase, t]).wait()

    @pl.loop(0, TAPS)
    def _(t):
        for phase, ref in enumerate(
            (pair_recv.at[t], plane_recv.at[t], line.at[t, 0:7], plane_recv.at[t], pair_recv.at[t])
        ):
            sent(ref, phase, t)


def store_kernel(*refs):
    sems = refs[6]
    copies = [pltpu.make_async_copy(refs[i], refs[i + 3], sems.at[i]) for i in range(3)]
    for copy in copies:
        copy.start()
    for copy in copies:
        copy.wait()


def local(inputs, weights, cotangent):
    scale = 1.0 / math.sqrt(ROWS * COLS * lax.axis_size("lat") * lax.axis_size("lon"))
    block = pltpu.VMEM((ROWS, COLS, CH), BF16)
    anywhere = pl.BlockSpec(memory_space=pl.ANY)
    dma = pltpu.SemaphoreType.DMA
    outputs, grad, kg = pl.pallas_call(
        functools.partial(kernel, scale),
        out_shape=(block, block, pltpu.VMEM((TAPS, 4, 4, 16, CH), F32)),
        in_specs=[anywhere] * 3,
        out_specs=(pl.BlockSpec(memory_space=pltpu.VMEM),) * 3,
        scratch_shapes=[
            pltpu.VMEM((ROWS, COLS, CH), BF16),
            pltpu.VMEM((ROWS, COLS, CH), BF16),
            pltpu.VMEM((3, 3, CH, CH), BF16),
            pltpu.VMEM((3, FLAT, CH), BF16),
            pltpu.VMEM((3, FLAT, CH), BF16),
            pltpu.VMEM((CH, DEPTH), BF16),
            pltpu.VMEM((2, COLS, CH), BF16),
            pltpu.VMEM((2, COLS, CH), BF16),
            pltpu.VMEM((3, 2, PITCH, CH), BF16),
            pltpu.VMEM((2, 2, ROWS, 1, CH), F32),
            pltpu.VMEM((2, 2, ROWS, 1, CH), F32),
            pltpu.VMEM((2, 2, 2, 1, CH), F32),
            pltpu.VMEM((2, 2, 2, 1, CH), F32),
            pltpu.VMEM((TAPS, 2, 4, 4, 16, 128), F32),
            pltpu.VMEM((TAPS, 4, 4, 16, 128), F32),
            pltpu.VMEM((TAPS, 4, 4, 16, 128), F32),
            pltpu.VMEM((TAPS, 15, 16, 128), F32),
            pltpu.VMEM((TAPS, NZ, 16, 128), F32),
            pltpu.VMEM((TAPS, 2, 4, 4, 16, 128), F32),
            dma((3,)),
            dma((2, 2)),
            dma((2, 2)),
            dma((2, 2)),
            dma((2, 2)),
            dma((2, 2)),
            dma((2, 2)),
            dma((5, TAPS)),
            dma((5, TAPS)),
        ],
        compiler_params=pltpu.CompilerParams(
            collective_id=0, has_side_effects=True, vmem_limit_bytes=56 * 2**20
        ),
        cost_estimate=pl.CostEstimate(flops=15 * 10**9, bytes_accessed=12 * 10**6, transcendentals=0),
    )(inputs, weights, cotangent)
    outputs, grad, kg = pl.pallas_call(
        store_kernel,
        out_shape=tuple(jax.ShapeDtypeStruct(v.shape, v.dtype) for v in (outputs, grad, kg)),
        in_specs=[anywhere] * 3,
        out_specs=(anywhere,) * 3,
        scratch_shapes=[dma((3,))],
        compiler_params=pltpu.CompilerParams(vmem_limit_bytes=2**20),
    )(outputs, grad, kg)
    return outputs, grad, kg.reshape(3, 3, CH, CH)


def solution(mesh):
    in_specs = (P("lat", "lon", None), P(), P("lat", "lon", None))
    out_specs = (P("lat", "lon", None), P("lat", "lon", None), P())
    return jax.shard_map(local, mesh=mesh, in_specs=in_specs, out_specs=out_specs, check_vma=False)
```

```python
import functools
import math

import jax
import jax.numpy as jnp
from jax import lax
from jax.experimental import pallas as pl
from jax.experimental.pallas import tpu as pltpu
from jax.sharding import PartitionSpec as P

MESH = pl.DeviceIdType.MESH
F32 = jnp.float32
BF16 = jnp.bfloat16

ROWS, COLS, CH = 90, 45, 256
PITCH = 48
FLAT = (ROWS + 2) * PITCH + 32
DEPTH = 4352
NX, NY, NZ = 4, 4, 8
TILE = 15
TILES = ROWS // TILE
TAPS = 9
WAITS = (2, 7, 11, 15, 17)
PLANE_ORDER = (10, 5, 15, 7, 13, 2, 8, 6, 9, 14, 11, 1, 4, 3, 12)
STEPS = TAPS + 2 * TILES


def rows_at(row, count):
    return pl.ds(pl.multiple_of(row * PITCH, 16), count)


def kernel(
    scale,
    x_hbm, w_hbm, c_hbm,
    out_v, grad_v, kg_v,
    x_in, c_in, w,
    xs, cs, xt, x_rows, c_rows, c_halo,
    col_send, col_recv, corner_send, corner_recv,
    term, pair_recv, half, plane_recv, line, final,
    load_sem,
    row_send_sem, row_recv_sem, col_send_sem, col_recv_sem, corner_send_sem, corner_recv_sem,
    ar_send_sem, ar_recv_sem,
):
    lat, lon = lax.axis_index("lat"), lax.axis_index("lon")
    x_hi, y = lat // 4, lat % 4
    x_lo, z, core = lon // 16, (lon // 2) % 8, lon % 2
    xc = x_hi * 2 + x_lo

    def device(xx, yy, zz, cc):
        return ((xx // 2) * 4 + yy, ((xx % 2) * 8 + zz) * 2 + cc)

    north, south = lat == 0, lat == 7
    across = (lon + 16) % 32
    up = (jnp.where(north, 0, lat - 1), jnp.where(north, across, lon))
    down = (jnp.where(south, 7, lat + 1), jnp.where(south, across, lon))
    left, right = (lat, (lon + 31) % 32), (lat, (lon + 1) % 32)
    other = device(xc, y, z, 1 - core)

    def plane_peer(d):
        return device((xc + d // 4) % NX, (y + d % 4) % NY, z, core)

    loads = [
        pltpu.make_async_copy(c_hbm, c_in, load_sem.at[0]),
        pltpu.make_async_copy(x_hbm, x_in, load_sem.at[1]),
        pltpu.make_async_copy(w_hbm, w, load_sem.at[2]),
    ]
    for load in loads:
        load.start()

    barrier = pltpu.get_barrier_semaphore()
    friends = [device(xc, y, (z + d) % NZ, core) for d in (4, 3, 5, 2, 6, 1, 7)]
    friends += [plane_peer(d) for d in range(1, 16)]
    friends += [up, down, left, right, other]
    for friend in friends:
        pl.semaphore_signal(barrier, inc=1, device_id=friend, device_id_type=MESH)
    pl.semaphore_wait(barrier, len(friends))

    def row_copies(which, source, target):
        to_up, to_down = jnp.where(north, 0, 1), jnp.where(south, 1, 0)
        return [
            pltpu.make_async_remote_copy(
                src_ref=source.at[0], dst_ref=target.at[to_up],
                send_sem=row_send_sem.at[which, 0], recv_sem=row_recv_sem.at[which, to_up],
                device_id=up, device_id_type=MESH,
            ),
            pltpu.make_async_remote_copy(
                src_ref=source.at[ROWS - 1], dst_ref=target.at[to_down],
                send_sem=row_send_sem.at[which, 1], recv_sem=row_recv_sem.at[which, to_down],
                device_id=down, device_id_type=MESH,
            ),
        ]

    def row_wait(which, target):
        for side in range(2):
            pltpu.make_async_copy(target.at[side], target.at[side], row_recv_sem.at[which, side]).wait()

    def col_copies(which):
        return [
            pltpu.make_async_remote_copy(
                src_ref=col_send.at[which, side], dst_ref=col_recv.at[which, side],
                send_sem=col_send_sem.at[which, side], recv_sem=col_recv_sem.at[which, side],
                device_id=to, device_id_type=MESH,
            )
            for side, to in ((0, right), (1, left))
        ]

    def corner_copies(which):
        return [
            pltpu.make_async_remote_copy(
                src_ref=corner_send.at[which, side], dst_ref=corner_recv.at[which, side],
                send_sem=corner_send_sem.at[which, side], recv_sem=corner_recv_sem.at[which, side],
                device_id=to, device_id_type=MESH,
            )
            for side, to in ((0, right), (1, left))
        ]

    def send_columns(which, block):
        for side, col in ((0, COLS - 1), (1, 0)):
            col_send[which, side] = block[:, col : col + 1, :].astype(F32)
            col_copies(which)[side].start()

    def send_corners(which, rows):
        for side, col in ((0, COLS - 1), (1, 0)):
            corner_send[which, side] = rows[:, col : col + 1, :].astype(F32)
            corner_copies(which)[side].start()

    def wait_corners(which):
        for side in range(2):
            pltpu.make_async_copy(
                corner_recv.at[which, side], corner_recv.at[which, side], corner_recv_sem.at[which, side]
            ).wait()

    def centred(row):
        return jnp.concatenate([row, jnp.zeros((PITCH - COLS, CH), BF16)], 0)

    def sideways(row, before, after):
        wide = row.astype(F32)
        pad = jnp.zeros((PITCH - COLS, CH), F32)
        return (
            (0, jnp.concatenate([before, wide, pad[1:]], 0).astype(BF16)),
            (2, jnp.concatenate([wide[1:], after, pad], 0).astype(BF16)),
        )

    def spread_centre(block, target):
        @pl.loop(0, ROWS, unroll=5)
        def _(r):
            target[1, rows_at(r + 1, PITCH), :] = centred(block[r])

        for b in range(3):
            target[b, 0:PITCH, :] = jnp.zeros((PITCH, CH), BF16)
            target[b, (ROWS + 1) * PITCH :, :] = jnp.zeros((FLAT - (ROWS + 1) * PITCH, CH), BF16)

    def spread_sides(which, block, target):
        for side in range(2):
            pltpu.make_async_copy(
                col_recv.at[which, side], col_recv.at[which, side], col_recv_sem.at[which, side]
            ).wait()

        @pl.loop(0, ROWS, unroll=5)
        def _(r):
            for b, value in sideways(block[r], col_recv[which, 0, r], col_recv[which, 1, r]):
                target[b, rows_at(r + 1, PITCH), :] = value

    def send_rows(which, block, rows):
        for copy in row_copies(which, block, rows):
            copy.start()

    loads[0].wait()
    send_rows(0, c_in, c_rows)
    send_columns(0, c_in)
    spread_centre(c_in, cs)
    loads[1].wait()
    spread_centre(x_in, xs)
    for i in range(DEPTH // 256):
        xt[:, i * 256 : (i + 1) * 256] = xs[1, PITCH + i * 256 : PITCH + (i + 1) * 256, :].T

    def tap_of(t):
        late = t - 5
        a_early = jnp.where(t == 1, 0, jnp.where(t == 2, 2, 1))
        b_early = jnp.where(t == 3, 0, jnp.where(t == 4, 2, 1))
        corner = t >= 5
        return (
            jnp.where(corner, (late // 2) * 2, a_early),
            jnp.where(corner, (late % 2) * 2, b_early),
        )

    top_tap = jnp.where(north, 0, 2)
    bottom_tap = jnp.where(south, 2, 0)

    def pair_copy(t):
        return pltpu.make_async_remote_copy(
            src_ref=term.at[t, 1 - core], dst_ref=pair_recv.at[t],
            send_sem=ar_send_sem.at[0, t], recv_sem=ar_recv_sem.at[0, t],
            device_id=other, device_id_type=MESH,
        )

    def remote(src, dst, phase, t, to):
        pltpu.make_async_remote_copy(
            src_ref=src, dst_ref=dst, send_sem=ar_send_sem.at[phase, t], recv_sem=ar_recv_sem.at[phase, t],
            device_id=to, device_id_type=MESH,
        ).start()

    def arrived(ref, phase, t):
        pltpu.make_async_copy(ref, ref, ar_recv_sem.at[phase, t]).wait()

    def to_plane(t):
        arrived(pair_recv.at[t], 0, t)
        half[t] = term[t, core] + pair_recv[t]
        for d in PLANE_ORDER:
            piece = half.at[t, (xc + d // 4) % NX, (y + d % 4) % NY]
            remote(piece, plane_recv.at[t, d - 1], 1, t, plane_peer(d))

    def to_line(t):
        arrived(plane_recv.at[t], 1, t)
        parts = [half[t, xc, y]] + [plane_recv[t, d] for d in range(15)]
        while len(parts) > 1:
            parts = [parts[i] + parts[i + 1] for i in range(0, len(parts), 2)]
        line[t, z] = parts[0]
        for d in (4, 3, 5, 2, 6, 1, 7):
            remote(line.at[t, z], line.at[t, z], 2, t, device(xc, y, (z + d) % NZ, core))

    def from_line(t):
        arrived(line.at[t, 0:7], 2, t)
        parts = [line[t, i] for i in range(NZ)]
        while len(parts) > 1:
            parts = [parts[i] + parts[i + 1] for i in range(0, len(parts), 2)]
        final[t, core, xc, y] = parts[0] * scale
        piece = final.at[t, core, xc, y]
        for d in PLANE_ORDER:
            remote(piece, piece, 3, t, plane_peer(d))

    def to_pair(t):
        arrived(plane_recv.at[t], 3, t)
        remote(final.at[t, core], final.at[t, core], 4, t, other)

    def finish(t):
        arrived(pair_recv.at[t], 4, t)
        a, b = tap_of(t)
        kg_v[a * 3 + b, :, :, :, :128] = final[t, 0]
        kg_v[a * 3 + b, :, :, :, 128:] = final[t, 1]

    plan = list(zip(WAITS, (to_plane, to_line, from_line, to_pair, finish)))

    def communicate(s, begin, end):
        for wait, phase in reversed(plan):
            if wait < end and TAPS + wait > begin:
                t = s - wait

                @pl.when((t >= 0) & (t < TAPS))
                def _():
                    phase(t)

    def weight_tap(t):
        a, b = tap_of(t)
        res = jnp.dot(xt[...], cs[2 - b, rows_at(2 - a, DEPTH), :], preferred_element_type=F32)
        term[t, 0] = res[:, :128].reshape(4, 4, 16, 128)
        term[t, 1] = res[:, 128:].reshape(4, 4, 16, 128)
        for side, tap, row in ((0, top_tap, 1), (1, bottom_tap, ROWS)):
            @pl.when(a == tap)
            def _():
                more = lax.dot_general(
                    xs[1, row * PITCH : row * PITCH + PITCH, :], c_halo[2 - b, side],
                    (((0,), (0,)), ((), ())), preferred_element_type=F32,
                )
                term[t, 0] += more[:, :128].reshape(4, 4, 16, 128)
                term[t, 1] += more[:, 128:].reshape(4, 4, 16, 128)
        pair_copy(t).start()

    def out_tile(i):
        acc = None
        for a in range(3):
            for b in range(3):
                part = jnp.dot(
                    xs[b, rows_at(i * TILE + a, TILE * PITCH), :], w[a, b], preferred_element_type=F32
                )
                acc = part if acc is None else acc + part
        out_v[pl.ds(i * TILE, TILE)] = acc.astype(BF16).reshape(TILE, PITCH, CH)[:, :COLS]

    def times_transposed(rows, weights):
        return lax.dot_general(rows, weights, (((1,), (1,)), ((), ())), preferred_element_type=F32)

    def grad_rows(row, count):
        acc = None
        for a in range(3):
            for b in range(3):
                part = times_transposed(cs[2 - b, rows_at(row + 2 - a, count * PITCH), :], w[a, b])
                acc = part if acc is None else acc + part
        return acc

    def grad_tile(i):
        grad_v[pl.ds(i * TILE, TILE)] = (
            grad_rows(i * TILE, TILE).astype(BF16).reshape(TILE, PITCH, CH)[:, :COLS]
        )
        for side, tile, row, tap in ((0, 0, 0, top_tap), (1, TILES - 1, ROWS - 1, bottom_tap)):
            @pl.when(i == tile)
            def _():
                acc = grad_rows(row, 1)
                for b in range(3):
                    acc = acc + times_transposed(c_halo[2 - b, side], w[tap, b])
                grad_v[row] = acc.astype(BF16)[:COLS]

    def edge_rows(which, rows):
        for end in range(2):
            for b, value in sideways(rows[end], corner_recv[which, 0, end], corner_recv[which, 1, end]):
                yield end, b, value

    @pl.loop(0, TAPS)
    def _(s):
        communicate(s, 0, TAPS)

        @pl.when(s == 1)
        def _():
            row_wait(0, c_rows)
            send_corners(0, c_rows)
            for end in range(2):
                c_halo[1, end] = centred(c_rows[end])
            send_rows(1, x_in, x_rows)

        @pl.when(s == 2)
        def _():
            send_columns(1, x_in)

        @pl.when(s == 6)
        def _():
            row_wait(1, x_rows)
            send_corners(1, x_rows)
            for end in range(2):
                place = slice(end * (ROWS + 1) * PITCH, end * (ROWS + 1) * PITCH + PITCH)
                xs[1, place, :] = centred(x_rows[end])

        @pl.when(s == 3)
        def _():
            spread_sides(0, c_in, cs)

        @pl.when(s == 5)
        def _():
            wait_corners(0)
            for end, b, value in edge_rows(0, c_rows):
                c_halo[b, end] = value

        weight_tap(s)

    loads[2].wait()
    spread_sides(1, x_in, xs)
    wait_corners(1)
    for end, b, value in edge_rows(1, x_rows):
        xs[b, end * (ROWS + 1) * PITCH : end * (ROWS + 1) * PITCH + PITCH, :] = value

    @pl.loop(TAPS, TAPS + TILES)
    def _(s):
        communicate(s, TAPS, TAPS + TILES)
        out_tile(s - TAPS)

    @pl.loop(TAPS + TILES, STEPS)
    def _(s):
        communicate(s, TAPS + TILES, STEPS)
        grad_tile(s - TAPS - TILES)

    for which, block, rows in ((0, c_in, c_rows), (1, x_in, x_rows)):
        for copy in row_copies(which, block, rows) + col_copies(which) + corner_copies(which):
            copy.wait_send()

    def sent(ref, phase, t):
        pltpu.make_async_copy(ref, ref, ar_send_sem.at[phase, t]).wait()

    @pl.loop(0, TAPS)
    def _(t):
        for phase, ref in enumerate((pair_recv.at[t], plane_recv.at[t], line.at[t, 0:7])):
            sent(ref, phase, t)

    last = TAPS + WAITS[-1]

    @pl.loop(STEPS, last)
    def _(s):
        communicate(s, STEPS, last)

    @pl.loop(0, TAPS)
    def _(t):
        sent(plane_recv.at[t], 3, t)
        sent(pair_recv.at[t], 4, t)


def store_kernel(*refs):
    sems = refs[6]
    copies = [pltpu.make_async_copy(refs[i], refs[i + 3], sems.at[i]) for i in range(3)]
    for copy in copies:
        copy.start()
    for copy in copies:
        copy.wait()


def local(inputs, weights, cotangent):
    scale = 1.0 / math.sqrt(ROWS * COLS * lax.axis_size("lat") * lax.axis_size("lon"))
    block = pltpu.VMEM((ROWS, COLS, CH), BF16)
    anywhere = pl.BlockSpec(memory_space=pl.ANY)
    dma = pltpu.SemaphoreType.DMA
    outputs, grad, kg = pl.pallas_call(
        functools.partial(kernel, scale),
        out_shape=(block, block, pltpu.VMEM((TAPS, 4, 4, 16, CH), F32)),
        in_specs=[anywhere] * 3,
        out_specs=(pl.BlockSpec(memory_space=pltpu.VMEM),) * 3,
        scratch_shapes=[
            pltpu.VMEM((ROWS, COLS, CH), BF16),
            pltpu.VMEM((ROWS, COLS, CH), BF16),
            pltpu.VMEM((3, 3, CH, CH), BF16),
            pltpu.VMEM((3, FLAT, CH), BF16),
            pltpu.VMEM((3, FLAT, CH), BF16),
            pltpu.VMEM((CH, DEPTH), BF16),
            pltpu.VMEM((2, COLS, CH), BF16),
            pltpu.VMEM((2, COLS, CH), BF16),
            pltpu.VMEM((3, 2, PITCH, CH), BF16),
            pltpu.VMEM((2, 2, ROWS, 1, CH), F32),
            pltpu.VMEM((2, 2, ROWS, 1, CH), F32),
            pltpu.VMEM((2, 2, 2, 1, CH), F32),
            pltpu.VMEM((2, 2, 2, 1, CH), F32),
            pltpu.VMEM((TAPS, 2, 4, 4, 16, 128), F32),
            pltpu.VMEM((TAPS, 4, 4, 16, 128), F32),
            pltpu.VMEM((TAPS, 4, 4, 16, 128), F32),
            pltpu.VMEM((TAPS, 15, 16, 128), F32),
            pltpu.VMEM((TAPS, NZ, 16, 128), F32),
            pltpu.VMEM((TAPS, 2, 4, 4, 16, 128), F32),
            dma((3,)),
            dma((2, 2)),
            dma((2, 2)),
            dma((2, 2)),
            dma((2, 2)),
            dma((2, 2)),
            dma((2, 2)),
            dma((5, TAPS)),
            dma((5, TAPS)),
        ],
        compiler_params=pltpu.CompilerParams(
            collective_id=0, has_side_effects=True, vmem_limit_bytes=56 * 2**20
        ),
        cost_estimate=pl.CostEstimate(flops=15 * 10**9, bytes_accessed=12 * 10**6, transcendentals=0),
    )(inputs, weights, cotangent)
    outputs, grad, kg = pl.pallas_call(
        store_kernel,
        out_shape=tuple(jax.ShapeDtypeStruct(v.shape, v.dtype) for v in (outputs, grad, kg)),
        in_specs=[anywhere] * 3,
        out_specs=(anywhere,) * 3,
        scratch_shapes=[dma((3,))],
        compiler_params=pltpu.CompilerParams(vmem_limit_bytes=2**20),
    )(outputs, grad, kg)
    return outputs, grad, kg.reshape(3, 3, CH, CH)


def solution(mesh):
    in_specs = (P("lat", "lon", None), P(), P("lat", "lon", None))
    out_specs = (P("lat", "lon", None), P("lat", "lon", None), P())
    return jax.shard_map(local, mesh=mesh, in_specs=in_specs, out_specs=out_specs, check_vma=False)
```
